32 devices in a mesh: groups: 2 (over y), tenant: 4 (over z), tensor: 4 (over x, core).
Axes of the slice: x: 2, y: 2, z: 4, core: 2. Of those that a mesh axis runs over, the one named last changes fastest.
Arguments:
- hidden_states: bfloat16 [512, 14336], P(('groups', 'tenant'), 'tensor'), parts along dimension 0, may hold values from -6 to 6
- tenant_ids: int32 [512], P(('groups', 'tenant')), parts along dimension 0, may hold values from 0 to 15, as said below
- owner_map: int32 [32], P('groups'), parts along dimension 0, may hold values from 0 to 15, as said below
- down_weight: bfloat16 [14336, 8192], P('tensor', 'tenant'), may hold values from -0.046875 to 0.046875
- adapter_down: bfloat16 [32, 14336, 64], P(('groups', 'tenant'), 'tensor'), parts along dimension 0, may hold values from -0.046875 to 0.046875
- adapter_up: bfloat16 [32, 64, 8192], P(('groups', 'tensor'), None, 'tenant'), parts along dimension 0, may hold values from -0.75 to 0.75
Outputs:
- layer_out: bfloat16 [512, 8192], P(('groups', 'tensor'), 'tenant'), parts along dimension 0
The draws below stay inside these ranges and needn't reach their ends.
There are 2 independent parts, one for each index of `groups`. The reference program is written for one: setup_inputs(seed, part) draws one part's arguments, and reference() takes and returns one part's arrays. A program takes and returns all parts, laid end to end along the dimension named above; an argument that names none is the same for every part. Nothing has to cross between parts.
Inputs may be any that keep to these rules, and one draw needn't show every extreme that they name: `tenant_ids`: in each aligned block of 64 rows, at most 32 rows have tenants whose slots lie in one range [o * 4, (o + 1) * 4); in every draw one such range gets exactly 32 rows from every block. `owner_map`: A permutation of the tenants.
All inputs are finite; a program needn't handle non-finite values.
Results may differ from the reference program's by a relative error of at most 0.004.
Values may be sent and summed in bfloat16 or wider, within the bound.
No kernel may reach another device: no remote copies, remote signals or barrier semaphores. Data moves between devices by JAX's collectives and lax.ppermute only.
A program may use at most 64 MiB of HBM per device.

```python
import jax
import jax.numpy as jnp
from jax import lax

D = 8192
FF = 14336
RANK = 64
TEN_DEV = 4
ROW_DEV = 64
TENANTS = 16
ROWS = 256
CAP = 32


def owner_table(key):
    return jax.random.permutation(jax.random.fold_in(key, 11), TENANTS).astype(jnp.int32)


def draw_owner_map(key, part):
    return owner_table(key)


def draw_tenant_ids(key, part):
    mapping = owner_table(key)
    key = jax.random.fold_in(key, 5)
    hot_key, blocks_key = jax.random.split(key, 2)
    owner_count = TENANTS // TEN_DEV
    hot_owner = jax.random.randint(hot_key, (), 0, owner_count).astype(jnp.int32)
    others = (hot_owner + 1 + jnp.arange(owner_count - 1, dtype=jnp.int32)) % owner_count
    pool_owners = jnp.repeat(others, CAP)

    def one_block(block_key):
        pool_key, mix_key, local_key = jax.random.split(block_key, 3)
        chosen = jax.random.permutation(pool_key, pool_owners)[:ROW_DEV - CAP]
        targets = jnp.concatenate([jnp.full((CAP,), hot_owner, jnp.int32), chosen])
        targets = jax.random.permutation(mix_key, targets)
        local_tenant = jax.random.randint(local_key, (ROW_DEV,), 0, TEN_DEV).astype(jnp.int32)
        return targets * TEN_DEV + local_tenant
    slot_ids = jax.vmap(one_block)(jax.random.split(blocks_key, ROWS // ROW_DEV)).reshape(-1)
    inverse = jnp.zeros((TENANTS,), jnp.int32).at[mapping].set(jnp.arange(TENANTS, dtype=jnp.int32))
    return inverse[slot_ids].astype(jnp.int32)


def block_levels(stream_key, shape, shards, least, high):
    def one(axis_at, blocks):
        heights = jax.random.uniform(jax.random.fold_in(jax.random.fold_in(stream_key, 6), axis_at), (blocks,), jnp.float32, least / len(shards), high / len(shards))
        return jnp.repeat(jnp.exp(heights), shape[axis_at] // blocks).reshape((-1,) + (1,) * (len(shape) - axis_at - 1))

    factor_of = one(*shards[0])
    for cut in shards[1:]:
        factor_of = factor_of * one(*cut)
    return factor_of


def normal_values(own_key, extent, width, reach, shards=(), held_as=jnp.bfloat16):
    entries = jax.random.normal(own_key, extent, jnp.float32) * width
    if len(shards) > 0:
        entries = block_levels(own_key, extent, shards, -0.22, 0.18) * entries
    return jnp.clip(entries, min=-reach, max=reach).astype(held_as)


def setup_inputs(seed: int = 0, part: int = 0) -> dict:
    streams_of = jax.random.split(jax.random.key(seed), 7)
    part_splits = jax.random.split(jax.random.fold_in(streams_of[6], part), 7)
    return {
        "hidden_states": normal_values(part_splits[0], (ROWS, FF), 1.0, 6.0, ((0, 4), (1, 4))),
        "tenant_ids": draw_tenant_ids(jax.random.fold_in(jax.random.fold_in(streams_of[6], part), 71), part),
        "owner_map": draw_owner_map(jax.random.fold_in(jax.random.fold_in(streams_of[6], part), 71), part),
        "down_weight": normal_values(streams_of[3], (FF, D), FF ** -0.5, 0.046875, ((0, 4), (1, 4))),
        "adapter_down": normal_values(part_splits[4], (TENANTS, FF, RANK), FF ** -0.5, 0.046875, ((0, 4), (1, 4))),
        "adapter_up": normal_values(part_splits[5], (TENANTS, RANK, D), RANK ** -0.5, 0.75, ((0, 4), (2, 4))),
    }


def reference(hidden_states, tenant_ids, owner_map, down_weight, adapter_down, adapter_up):
    slot_ids = owner_map[tenant_ids].astype(jnp.int32)
    base_part = jnp.dot(hidden_states, down_weight, preferred_element_type=jnp.float32)
    group_rows = 16

    def adapt_block(inputs):
        row_block, block_slots = inputs
        down_rows = adapter_down[block_slots].astype(jnp.float32)
        reduced = jnp.einsum("rf,rfk->rk", row_block.astype(jnp.float32), down_rows).astype(jnp.bfloat16)
        up_rows = adapter_up[block_slots].astype(jnp.float32)
        return jnp.einsum("rk,rkd->rd", reduced.astype(jnp.float32), up_rows)

    delta = lax.map(adapt_block, (hidden_states.reshape(-1, group_rows, FF), slot_ids.reshape(-1, group_rows)))
    delta = delta.reshape(ROWS, D)
    return (base_part + delta).astype(jnp.bfloat16)
```

```python
import jax
import jax.numpy as jnp
from jax import lax
from jax.sharding import PartitionSpec as P


def lookup(row_ids, mapping):
    matches = row_ids[:, None] == jnp.arange(mapping.shape[0], dtype=jnp.int32)[None, :]
    return jnp.sum(jnp.where(matches, mapping[None, :], 0), axis=1)


def on_device_general(hidden_states, tenant_ids, owner_map, down_weight, adapter_down, adapter_up):
    rows_dev = hidden_states.shape[0]
    ten_dev = adapter_down.shape[0]
    low_rank = adapter_down.shape[2]
    per_group = adapter_up.shape[0]
    cols_dev = adapter_up.shape[2]
    owners = lax.axis_size("tenant")
    capacity = min(4 * rows_dev // owners, rows_dev // 2)
    slot_limit = owners * capacity
    me_group = lax.axis_index("tensor")
    everyone, all_ids = (
        lax.all_gather(hidden_states, "tenant", axis=0, tiled=True),
        lax.all_gather(tenant_ids, "tenant", axis=0, tiled=True),
    )
    total_rows = everyone.shape[0]
    all_slots = lookup(all_ids, owner_map)
    my_slots = lookup(tenant_ids, owner_map)
    target = my_slots // ten_dev
    onehot = (target[:, None] == jnp.arange(owners, dtype=jnp.int32)[None, :]).astype(jnp.int32)
    position = jnp.sum(jnp.cumsum(onehot, axis=0) * onehot, axis=1) - 1
    slot_cell = target * capacity + position
    select = slot_cell[None, :] == jnp.arange(slot_limit, dtype=jnp.int32)[:, None]
    outgoing = jnp.dot(
        select.astype(jnp.bfloat16), hidden_states, preferred_element_type=jnp.float32
    )
    outgoing = outgoing.astype(jnp.bfloat16).reshape(owners, capacity, hidden_states.shape[1])
    local_tags = jnp.sum(jnp.where(select, (my_slots % ten_dev)[None, :], 0), axis=1)
    local_tags = jnp.where(jnp.any(select, axis=1), local_tags, -1).reshape(owners, capacity)
    payload = lax.all_to_all(outgoing, "tenant", split_axis=0, concat_axis=0, tiled=True)
    project_local_tags = lax.all_to_all(
        local_tags, "tenant", split_axis=0, concat_axis=0, tiled=True
    )
    flattened = payload.reshape(-1, payload.shape[2])
    mixed = jnp.einsum("nf,tfk->ntk", flattened, adapter_down, preferred_element_type=jnp.float32)
    chosen = (
        project_local_tags.reshape(-1)[:, None] == jnp.arange(ten_dev, dtype=jnp.int32)[None, :]
    )
    result = jnp.sum(jnp.where(chosen[:, :, None], mixed, 0.0), axis=1)
    partial_value = result.reshape(payload.shape[0], payload.shape[1], low_rank)
    summed = lax.psum(partial_value, "tensor")
    reduced = lax.all_to_all(
        summed.astype(jnp.bfloat16), "tenant", split_axis=0, concat_axis=0, tiled=True
    )
    my_low = jnp.dot(
        select.T.astype(jnp.bfloat16),
        reduced.reshape(-1, low_rank),
        preferred_element_type=jnp.float32,
    )
    all_low = lax.all_gather(my_low.astype(jnp.bfloat16), "tenant", axis=0, tiled=True)
    first_slot = me_group * per_group
    group_index = all_slots - first_slot
    chosen_group = group_index[:, None] == jnp.arange(per_group, dtype=jnp.int32)[None, :]
    spread = jnp.where(chosen_group[:, :, None], all_low[:, None, :], jnp.zeros((), jnp.bfloat16))
    spread = spread.reshape(total_rows, per_group * low_rank)
    up_flat = adapter_up.reshape(per_group * low_rank, cols_dev)
    layer_out = lax.psum_scatter(
        jnp.dot(everyone, down_weight, preferred_element_type=jnp.float32),
        "tensor",
        scatter_dimension=0,
        tiled=True,
    )
    layer_out = layer_out + lax.psum_scatter(
        jnp.dot(spread, up_flat, preferred_element_type=jnp.float32),
        "tensor",
        scatter_dimension=0,
        tiled=True,
    )
    return layer_out.astype(jnp.bfloat16)


def ordered(first, then):
    return lax.optimization_barrier((first, then))


def on_device_4x4(hidden_states, tenant_ids, owner_map, down_weight, adapter_down, adapter_up):
    rows_dev = hidden_states.shape[0]
    ten_dev, _, low_rank = adapter_down.shape
    wide = ten_dev * low_rank
    t = lax.axis_index("tenant")
    q = lax.axis_index("tensor")
    bf16, f32 = jnp.bfloat16, jnp.float32

    def along(name, pairs):
        return lambda value: lax.ppermute(value, name, pairs)

    outer_pairs = along("tenant", [(0, 1), (1, 0), (2, 3), (3, 2)])
    two_apart = along("tenant", [(0, 2), (2, 0), (1, 3), (3, 1)])
    inner_pair = along("tenant", [(1, 2), (2, 1)])
    to_ends = along("tenant", [(2, 3), (1, 0)])
    opposite = along("tenant", [(0, 3), (3, 0), (1, 2), (2, 1)])
    cores = along("tensor", [(0, 1), (1, 0), (2, 3), (3, 2)])
    chips = along("tensor", [(0, 2), (2, 0), (1, 3), (3, 1)])

    from_two = two_apart(hidden_states)
    from_pair = outer_pairs(hidden_states)
    up_chip = chips(adapter_up)
    home_ids = lax.ppermute(
        tenant_ids,
        ("tenant", "tensor"),
        [(a * 4 + b, b * 4 + a) for a in range(4) for b in range(4)],
    )
    from_two, hidden_late = ordered(from_two, hidden_states)
    from_end = to_ends(from_two)
    from_inner = inner_pair(hidden_late)
    inside = (t == 1) | (t == 2)
    from_last = jnp.where(inside, from_inner, from_end)

    down_flat = jnp.transpose(adapter_down, (1, 0, 2)).reshape(-1, wide)

    def dot(a, b):
        return jnp.dot(a, b, preferred_element_type=f32)

    blocks = (hidden_states, from_pair, from_two, from_last)
    low = [dot(rows, down_flat) for rows in blocks]
    base = [dot(rows, down_weight) for rows in blocks]

    core = q % 2
    even = (t % 2) == core
    near = (t // 2) == (q // 2)

    def to_home(parts, sent):
        keep = [jnp.where(even, parts[i], parts[i + 1]) for i in (0, 2)]
        give = [jnp.where(even, parts[i + 1], parts[i]).astype(sent) for i in (0, 2)]
        got = [cores(value) for value in give]
        both = [a + b.astype(f32) for a, b in zip(keep, got)]
        mine = jnp.where(near, both[0], both[1])
        other = jnp.where(near, both[1], both[0]).astype(sent)
        return mine + chips(other).astype(f32)

    reduced = to_home(low, f32).astype(bf16)
    by_owner = (reduced, outer_pairs(reduced), two_apart(reduced), opposite(reduced))

    up_core = cores(adapter_up)
    up_both = cores(up_chip)
    ups = ((q, adapter_up), (q ^ 2, up_chip), (q ^ 1, up_core), (q ^ 3, up_both))

    slots = lookup(home_ids, owner_map)
    lane = jnp.arange(wide, dtype=jnp.int32)[None, :] // low_rank
    zero = jnp.zeros((), bf16)
    chosen = zero
    for step, value in enumerate(by_owner):
        first = (t ^ step) * ten_dev
        chosen = chosen + jnp.where(slots[:, None] - first == lane, value, zero)
    row = sum(chosen[:, i * low_rank : (i + 1) * low_rank] for i in range(ten_dev))
    tiled = jnp.concatenate([row] * ten_dev, axis=1)
    delta = 0.0
    for index, up in ups:
        spread = jnp.where(slots[:, None] - index * ten_dev == lane, tiled, zero)
        delta = delta + dot(spread, up.reshape(wide, -1))
    return (to_home(base, bf16) + delta).astype(bf16)


def solution(mesh):
    small = mesh.shape["tenant"] == 4 and mesh.shape["tensor"] == 4
    return jax.shard_map(
        on_device_4x4 if small else on_device_general,
        mesh=mesh,
        in_specs=(
            P(("groups", "tenant"), "tensor"),
            P(("groups", "tenant")),
            P("groups"),
            P("tensor", "tenant"),
            P(("groups", "tenant"), "tensor", None),
            P(("groups", "tensor"), None, "tenant"),
        ),
        out_specs=P(("groups", "tensor"), "tenant"),
        check_vma=False,
    )
```

```python
import functools

import jax
import jax.numpy as jnp
from jax import lax
from jax.experimental import pallas as pl
from jax.experimental.pallas import tpu as pltpu
from jax.sharding import PartitionSpec as P


def lookup(row_ids, mapping):
    matches = row_ids[:, None] == jnp.arange(mapping.shape[0], dtype=jnp.int32)[None, :]
    return jnp.sum(jnp.where(matches, mapping[None, :], 0), axis=1)


def on_device_general(hidden_states, tenant_ids, owner_map, down_weight, adapter_down, adapter_up):
    rows_dev = hidden_states.shape[0]
    ten_dev = adapter_down.shape[0]
    low_rank = adapter_down.shape[2]
    per_group = adapter_up.shape[0]
    cols_dev = adapter_up.shape[2]
    owners = lax.axis_size("tenant")
    capacity = min(4 * rows_dev // owners, rows_dev // 2)
    slot_limit = owners * capacity
    me_group = lax.axis_index("tensor")
    everyone, all_ids = (
        lax.all_gather(hidden_states, "tenant", axis=0, tiled=True),
        lax.all_gather(tenant_ids, "tenant", axis=0, tiled=True),
    )
    total_rows = everyone.shape[0]
    all_slots = lookup(all_ids, owner_map)
    my_slots = lookup(tenant_ids, owner_map)
    target = my_slots // ten_dev
    onehot = (target[:, None] == jnp.arange(owners, dtype=jnp.int32)[None, :]).astype(jnp.int32)
    position = jnp.sum(jnp.cumsum(onehot, axis=0) * onehot, axis=1) - 1
    slot_cell = target * capacity + position
    select = slot_cell[None, :] == jnp.arange(slot_limit, dtype=jnp.int32)[:, None]
    outgoing = jnp.dot(
        select.astype(jnp.bfloat16), hidden_states, preferred_element_type=jnp.float32
    )
    outgoing = outgoing.astype(jnp.bfloat16).reshape(owners, capacity, hidden_states.shape[1])
    local_tags = jnp.sum(jnp.where(select, (my_slots % ten_dev)[None, :], 0), axis=1)
    local_tags = jnp.where(jnp.any(select, axis=1), local_tags, -1).reshape(owners, capacity)
    payload = lax.all_to_all(outgoing, "tenant", split_axis=0, concat_axis=0, tiled=True)
    project_local_tags = lax.all_to_all(
        local_tags, "tenant", split_axis=0, concat_axis=0, tiled=True
    )
    flattened = payload.reshape(-1, payload.shape[2])
    mixed = jnp.einsum("nf,tfk->ntk", flattened, adapter_down, preferred_element_type=jnp.float32)
    chosen = (
        project_local_tags.reshape(-1)[:, None] == jnp.arange(ten_dev, dtype=jnp.int32)[None, :]
    )
    result = jnp.sum(jnp.where(chosen[:, :, None], mixed, 0.0), axis=1)
    partial_value = result.reshape(payload.shape[0], payload.shape[1], low_rank)
    summed = lax.psum(partial_value, "tensor")
    reduced = lax.all_to_all(
        summed.astype(jnp.bfloat16), "tenant", split_axis=0, concat_axis=0, tiled=True
    )
    my_low = jnp.dot(
        select.T.astype(jnp.bfloat16),
        reduced.reshape(-1, low_rank),
        preferred_element_type=jnp.float32,
    )
    all_low = lax.all_gather(my_low.astype(jnp.bfloat16), "tenant", axis=0, tiled=True)
    first_slot = me_group * per_group
    group_index = all_slots - first_slot
    chosen_group = group_index[:, None] == jnp.arange(per_group, dtype=jnp.int32)[None, :]
    spread = jnp.where(chosen_group[:, :, None], all_low[:, None, :], jnp.zeros((), jnp.bfloat16))
    spread = spread.reshape(total_rows, per_group * low_rank)
    up_flat = adapter_up.reshape(per_group * low_rank, cols_dev)
    layer_out = lax.psum_scatter(
        jnp.dot(everyone, down_weight, preferred_element_type=jnp.float32),
        "tensor",
        scatter_dimension=0,
        tiled=True,
    )
    layer_out = layer_out + lax.psum_scatter(
        jnp.dot(spread, up_flat, preferred_element_type=jnp.float32),
        "tensor",
        scatter_dimension=0,
        tiled=True,
    )
    return layer_out.astype(jnp.bfloat16)


def dot(a, b):
    return jnp.dot(a, b, preferred_element_type=jnp.float32)


def dot_t(a, b):
    return lax.dot_general(a, b, (((1,), (1,)), ((), ())), preferred_element_type=jnp.float32)


CHEAP = pl.CostEstimate(flops=1, bytes_accessed=1, transcendentals=0)
HERE = pl.BlockSpec(memory_space=pltpu.VMEM)
TILE = 256


def call(kernel, outs, *operands, scratch=()):
    return pl.pallas_call(
        kernel,
        in_specs=[HERE] * len(operands),
        out_specs=[HERE] * len(outs),
        out_shape=list(outs),
        scratch_shapes=list(scratch),
        cost_estimate=CHEAP,
        compiler_params=pltpu.CompilerParams(vmem_limit_bytes=8 * 2**20),
    )(*operands)


def tiles(length):
    return [slice(i, i + TILE) for i in range(0, length, TILE)]


def is_even():
    return lax.axis_index("tenant") % 2 == lax.axis_index("tensor") % 2


def is_near():
    return lax.axis_index("tenant") // 2 == lax.axis_index("tensor") // 2


def arrived(end, inner):
    t = lax.axis_index("tenant")
    return jnp.where((t == 1) | (t == 2), inner[...], end[...])


def own_kernel(x, w, down, base0, low0, a, b):
    half = a.shape[1]
    a[...] = x[:, :half]
    b[...] = x[:, half:]
    low0[...] = dot_t(x[...], down[...])
    for part in tiles(w.shape[1]):
        base0[:, part] = dot(x[...], w[:, part])


def middle_kernel(pair, two_a, two_b, w, down, base0, low0, ids, *outs):
    give, keep, base2, low_give, low_keep, low2, ids_held, both = outs
    ids_held[...] = ids[...]
    rows, half = two_a.shape
    even = is_even()
    both[:rows] = pair[...]
    both[rows:, :half] = two_a[...]
    both[rows:, half:] = two_b[...]
    low = dot_t(both[...], down[...])
    low_keep[...] = jnp.where(even, low0[...], low[:rows])
    low_give[...] = jnp.where(even, low[:rows], low0[...])
    low2[...] = low[rows:]
    for part in tiles(w.shape[1]):
        got = dot(both[...], w[:, part])
        base1 = got[:rows]
        base2[:, part] = got[rows:]
        keep[:, part] = jnp.where(even, base0[:, part], base1)
        give[:, part] = jnp.where(even, base1, base0[:, part]).astype(give.dtype)


def early_kernel(end, inner, w, down, base2, low2, early, low):
    del base2
    rows, half = end.shape
    x = arrived(end, inner)
    low[:rows] = low2[...]
    low[rows:] = dot_t(x, down[:, :half])
    for part in tiles(w.shape[1]):
        early[:, part] = dot(x, w[:half, part])


def low_kernel(end, inner, down, low, keep0, got0, give, keep, both0):
    rows, half = end.shape
    even = is_even()
    low2 = low[:rows]
    low3 = low[rows:] + dot_t(arrived(end, inner), down[:, half:])
    keep[...] = jnp.where(even, low2, low3)
    give[...] = jnp.where(even, low3, low2)
    both0[...] = keep0[...] + got0[...]


def late_kernel(end, inner, w, early, base2, keep0, got0, slots, low_got, give, keep, both0):
    del slots, low_got
    half = end.shape[1]
    x = arrived(end, inner)
    even = is_even()
    for part in tiles(w.shape[1]):
        base3 = early[:, part] + dot(x, w[half:, part])
        keep[:, part] = jnp.where(even, base2[:, part], base3)
        give[:, part] = jnp.where(even, base3, base2[:, part]).astype(give.dtype)
        both0[:, part] = keep0[:, part] + got0[:, part].astype(jnp.float32)


def chip_sum_kernel(both0, keep1, got1, mine, other):
    near = is_near()
    for part in tiles(mine.shape[1]):
        both1 = keep1[:, part] + got1[:, part].astype(jnp.float32)
        mine[:, part] = jnp.where(near, both0[:, part], both1)
        other[:, part] = jnp.where(near, both1, both0[:, part]).astype(other.dtype)


def base_sum_kernel(both0, keep1, got1, low_got, mine, other):
    del low_got
    chip_sum_kernel(both0, keep1, got1, mine, other)


def low_sum_kernel(both0, keep1, got1, up, mine, other, up_held):
    chip_sum_kernel(both0, keep1, got1, mine, other)
    up_held[...] = up[...]


def lanes(shape, low_rank):
    position = lax.broadcasted_iota(jnp.int32, shape, 1)
    starts = range(low_rank, shape[1], low_rank)
    return sum((position >= start).astype(jnp.int32) for start in starts)


def reduced_kernel(low_rank, mine, got, slots, out):
    ten_dev = slots.shape[1] // low_rank
    here = slots[...] - lax.axis_index("tenant") * ten_dev == lanes(slots.shape, low_rank)
    out[...] = jnp.where(here, mine[...] + got[...], 0.0).astype(out.dtype)


def delta_kernel(low_rank, slots, reduced0, reduced1, up0, up1, up2, up3, mine, out):
    q = lax.axis_index("tensor")
    f32, bf16 = jnp.float32, jnp.bfloat16
    wide = slots.shape[1]
    ten_dev = wide // low_rank
    lane = lanes(slots.shape, low_rank)
    i = lax.broadcasted_iota(jnp.int32, (wide, wide), 0)
    j = lax.broadcasted_iota(jnp.int32, (wide, wide), 1)
    same = jnp.zeros((wide, wide), f32)
    for shift in range(-wide + low_rank, wide, low_rank):
        same = jnp.where(i - j == shift, 1.0, same)
    spread = dot((reduced0[...].astype(f32) + reduced1[...].astype(f32)).astype(bf16), same.astype(bf16))
    terms = []
    for step, up in zip((0, 2, 1, 3), (up0, up1, up2, up3)):
        here = slots[...] - (q ^ step) * ten_dev == lane
        terms.append((jnp.where(here, spread, 0.0).astype(bf16), up))
    for part in tiles(mine.shape[1]):
        total = mine[:, part]
        for rows, up in terms:
            total = total + dot(rows, up[:, part])
        out[:, part] = total


def on_device_4x4(hidden_states, tenant_ids, owner_map, down_weight, adapter_down, adapter_up):
    rows, depth = hidden_states.shape
    cols = down_weight.shape[1]
    half = depth // 2
    ten_dev, _, low_rank = adapter_down.shape
    wide = ten_dev * low_rank
    bf16, f32 = jnp.bfloat16, jnp.float32

    def along(name, pairs):
        return lambda value: lax.ppermute(value, name, pairs)

    outer_pairs = along("tenant", [(0, 1), (1, 0), (2, 3), (3, 2)])
    two_apart = along("tenant", [(0, 2), (2, 0), (1, 3), (3, 1)])
    inner_pair = along("tenant", [(1, 2), (2, 1)])
    to_ends = along("tenant", [(2, 3), (1, 0)])
    opposite = along("tenant", [(0, 3), (3, 0), (1, 2), (2, 1)])
    cores = along("tensor", [(0, 1), (1, 0), (2, 3), (3, 2)])
    chips = along("tensor", [(0, 2), (2, 0), (1, 3), (3, 1)])

    def out(shape, dtype=f32):
        return jax.ShapeDtypeStruct(shape, dtype)

    tall, flat, part = (rows, cols), (rows, wide), (rows, half)

    two = [two_apart(hidden_states[:, :half]), two_apart(hidden_states[:, half:])]
    pair = outer_pairs(hidden_states)
    up0 = adapter_up.reshape(wide, cols)
    up1 = chips(up0)
    down = jnp.transpose(adapter_down, (0, 2, 1)).reshape(wide, depth)
    base0, low0, *own = call(
        own_kernel,
        [out(tall), out(flat), out(part, bf16), out(part, bf16)],
        hidden_states, down_weight, down,
    )
    end = [to_ends(value) for value in two]
    inner = [inner_pair(value) for value in own]
    give0, keep0, base2, low_give0, low_keep0, low2, ids = call(
        middle_kernel,
        [out(tall, bf16), out(tall), out(tall)] + [out(flat)] * 3 + [out((1, rows), jnp.int32)],
        pair, *two, down_weight, down, base0, low0, tenant_ids[None],
        scratch=[pltpu.VMEM((2 * rows, depth), bf16)],
    )
    home_ids = lax.ppermute(
        ids,
        ("tenant", "tensor"),
        [(a * 4 + b, b * 4 + a) for a in range(4) for b in range(4)],
    )
    slots = jnp.broadcast_to(lookup(home_ids[0], owner_map)[:, None], flat)
    early, low = call(
        early_kernel,
        [out(tall), out((2 * rows, wide))],
        end[0], inner[0], down_weight, down, base2, low2,
    )
    low_give1, low_keep1, low_both0 = call(
        low_kernel, [out(flat)] * 3, end[1], inner[1], down, low, low_keep0, cores(low_give0)
    )
    low_got1 = cores(low_give1)
    low_mine, low_other, up_held = call(
        low_sum_kernel,
        [out(flat)] * 2 + [out((wide, cols), bf16)],
        low_both0, low_keep1, low_got1, up1,
    )
    give1, keep1, both0 = call(
        late_kernel,
        [out(tall, bf16), out(tall), out(tall)],
        end[1], inner[1], down_weight, early, base2, keep0, cores(give0), slots, low_got1,
    )
    low_from_chip = chips(low_other)
    mine, other = call(
        base_sum_kernel,
        [out(tall), out(tall, bf16)],
        both0, keep1, cores(give1), low_from_chip,
    )
    from_chip = chips(other)
    (reduced,) = call(
        functools.partial(reduced_kernel, low_rank),
        [out(flat, bf16)],
        low_mine, low_from_chip, slots,
    )
    reduced = reduced + outer_pairs(reduced)
    (total,) = call(
        functools.partial(delta_kernel, low_rank),
        [out(tall)],
        slots, reduced, two_apart(reduced), up0, up1, cores(up0), cores(up_held), mine,
    )
    return (total + from_chip.astype(f32)).astype(bf16)


def solution(mesh):
    small = mesh.shape["tenant"] == 4 and mesh.shape["tensor"] == 4
    return jax.shard_map(
        on_device_4x4 if small else on_device_general,
        mesh=mesh,
        in_specs=(
            P(("groups", "tenant"), "tensor"),
            P(("groups", "tenant")),
            P("groups"),
            P("tensor", "tenant"),
            P(("groups", "tenant"), "tensor", None),
            P(("groups", "tensor"), None, "tenant"),
        ),
        out_specs=P(("groups", "tensor"), "tenant"),
        check_vma=False,
    )
```

```python
import functools

import jax
import jax.numpy as jnp
from jax import lax
from jax.experimental import pallas as pl
from jax.experimental.pallas import tpu as pltpu
from jax.sharding import PartitionSpec as P


def lookup(row_ids, mapping):
    matches = row_ids[:, None] == jnp.arange(mapping.shape[0], dtype=jnp.int32)[None, :]
    return jnp.sum(jnp.where(matches, mapping[None, :], 0), axis=1)


def on_device_general(hidden_states, tenant_ids, owner_map, down_weight, adapter_down, adapter_up):
    rows_dev = hidden_states.shape[0]
    ten_dev = adapter_down.shape[0]
    low_rank = adapter_down.shape[2]
    per_group = adapter_up.shape[0]
    cols_dev = adapter_up.shape[2]
    owners = lax.axis_size("tenant")
    capacity = min(4 * rows_dev // owners, rows_dev // 2)
    slot_limit = owners * capacity
    me_group = lax.axis_index("tensor")
    everyone, all_ids = (
        lax.all_gather(hidden_states, "tenant", axis=0, tiled=True),
        lax.all_gather(tenant_ids, "tenant", axis=0, tiled=True),
    )
    total_rows = everyone.shape[0]
    all_slots = lookup(all_ids, owner_map)
    my_slots = lookup(tenant_ids, owner_map)
    target = my_slots // ten_dev
    onehot = (target[:, None] == jnp.arange(owners, dtype=jnp.int32)[None, :]).astype(jnp.int32)
    position = jnp.sum(jnp.cumsum(onehot, axis=0) * onehot, axis=1) - 1
    slot_cell = target * capacity + position
    select = slot_cell[None, :] == jnp.arange(slot_limit, dtype=jnp.int32)[:, None]
    outgoing = jnp.dot(
        select.astype(jnp.bfloat16), hidden_states, preferred_element_type=jnp.float32
    )
    outgoing = outgoing.astype(jnp.bfloat16).reshape(owners, capacity, hidden_states.shape[1])
    local_tags = jnp.sum(jnp.where(select, (my_slots % ten_dev)[None, :], 0), axis=1)
    local_tags = jnp.where(jnp.any(select, axis=1), local_tags, -1).reshape(owners, capacity)
    payload = lax.all_to_all(outgoing, "tenant", split_axis=0, concat_axis=0, tiled=True)
    project_local_tags = lax.all_to_all(
        local_tags, "tenant", split_axis=0, concat_axis=0, tiled=True
    )
    flattened = payload.reshape(-1, payload.shape[2])
    mixed = jnp.einsum("nf,tfk->ntk", flattened, adapter_down, preferred_element_type=jnp.float32)
    chosen = (
        project_local_tags.reshape(-1)[:, None] == jnp.arange(ten_dev, dtype=jnp.int32)[None, :]
    )
    result = jnp.sum(jnp.where(chosen[:, :, None], mixed, 0.0), axis=1)
    partial_value = result.reshape(payload.shape[0], payload.shape[1], low_rank)
    summed = lax.psum(partial_value, "tensor")
    reduced = lax.all_to_all(
        summed.astype(jnp.bfloat16), "tenant", split_axis=0, concat_axis=0, tiled=True
    )
    my_low = jnp.dot(
        select.T.astype(jnp.bfloat16),
        reduced.reshape(-1, low_rank),
        preferred_element_type=jnp.float32,
    )
    all_low = lax.all_gather(my_low.astype(jnp.bfloat16), "tenant", axis=0, tiled=True)
    first_slot = me_group * per_group
    group_index = all_slots - first_slot
    chosen_group = group_index[:, None] == jnp.arange(per_group, dtype=jnp.int32)[None, :]
    spread = jnp.where(chosen_group[:, :, None], all_low[:, None, :], jnp.zeros((), jnp.bfloat16))
    spread = spread.reshape(total_rows, per_group * low_rank)
    up_flat = adapter_up.reshape(per_group * low_rank, cols_dev)
    layer_out = lax.psum_scatter(
        jnp.dot(everyone, down_weight, preferred_element_type=jnp.float32),
        "tensor",
        scatter_dimension=0,
        tiled=True,
    )
    layer_out = layer_out + lax.psum_scatter(
        jnp.dot(spread, up_flat, preferred_element_type=jnp.float32),
        "tensor",
        scatter_dimension=0,
        tiled=True,
    )
    return layer_out.astype(jnp.bfloat16)


def dot(a, b):
    return jnp.dot(a, b, preferred_element_type=jnp.float32)


def dot_t(a, b):
    return lax.dot_general(a, b, (((1,), (1,)), ((), ())), preferred_element_type=jnp.float32)


LATE = 2**23
CHEAP = pl.CostEstimate(flops=1, bytes_accessed=1, transcendentals=0)
HERE = pl.BlockSpec(memory_space=pltpu.VMEM)
TILE = 256


def call(kernel, outs, *operands, scratch=(), cost=CHEAP):
    return pl.pallas_call(
        kernel,
        in_specs=[HERE] * len(operands),
        out_specs=[HERE] * len(outs),
        out_shape=list(outs),
        scratch_shapes=list(scratch),
        cost_estimate=cost,
        compiler_params=pltpu.CompilerParams(vmem_limit_bytes=8 * 2**20),
    )(*operands)


def tiles(length):
    return [slice(i, i + TILE) for i in range(0, length, TILE)]


def is_even():
    return lax.axis_index("tenant") % 2 == lax.axis_index("tensor") % 2


def is_near():
    return lax.axis_index("tenant") // 2 == lax.axis_index("tensor") // 2


def arrived(end, inner):
    t = lax.axis_index("tenant")
    return jnp.where((t == 1) | (t == 2), inner[...], end[...])


def own_kernel(x, w, down, base0, low0, a, b):
    half = a.shape[1]
    a[...] = x[:, :half]
    b[...] = x[:, half:]
    low0[...] = dot_t(x[...], down[...])
    for part in tiles(w.shape[1]):
        base0[:, part] = dot(x[...], w[:, part])


def middle_kernel(pair, two_a, two_b, w, down, base1, base2, low, both):
    rows, half = two_a.shape
    both[:rows] = pair[...]
    both[rows:, :half] = two_a[...]
    both[rows:, half:] = two_b[...]
    low[...] = dot_t(both[...], down[...])
    for part in tiles(w.shape[1]):
        got = dot(both[...], w[:, part])
        base1[:, part] = got[:rows]
        base2[:, part] = got[rows:]


def early_kernel(end, inner, w, down, base2, low12, early, low_early):
    del base2
    rows, half = end.shape
    x = arrived(end, inner)
    low_early[:rows] = low12[rows:]
    low_early[rows:] = dot_t(x, down[:, :half])
    for part in tiles(w.shape[1]):
        early[:, part] = dot(x, w[:half, part])


def pick(blocks, part, give, keep):
    even = is_even()
    rows = blocks[0].shape[0]
    for at in (0, 1):
        first, second = blocks[2 * at], blocks[2 * at + 1]
        target = slice(at * rows, (at + 1) * rows)
        keep[target, part] = jnp.where(even, first, second)
        give[target, part] = jnp.where(even, second, first).astype(give.dtype)


def low_kernel(end, inner, down, low0, low12, low_early, give, keep):
    rows, half = end.shape
    low3 = low_early[rows:] + dot_t(arrived(end, inner), down[:, half:])
    blocks = (low0[...], low12[:rows], low_early[:rows], low3)
    pick(blocks, slice(None), give, keep)


def late_kernel(end, inner, w, early, low_give, base3):
    del low_give
    half = end.shape[1]
    x = arrived(end, inner)
    for part in tiles(w.shape[1]):
        base3[:, part] = early[:, part] + dot(x, w[half:, part])


def pick_kernel(base0, base1, base2, base3, low_other, give, keep):
    del low_other
    for part in tiles(base0.shape[1]):
        pick([block[:, part] for block in (base0, base1, base2, base3)], part, give, keep)


def chip_sum_kernel(keep, got, mine, other):
    near = is_near()
    rows = mine.shape[0]
    for part in tiles(mine.shape[1]):
        both = keep[:, part] + got[:, part].astype(jnp.float32)
        mine[:, part] = jnp.where(near, both[:rows], both[rows:])
        other[:, part] = jnp.where(near, both[rows:], both[:rows]).astype(other.dtype)


def low_sum_kernel(keep, got, base3, mine, other):
    del base3
    chip_sum_kernel(keep, got, mine, other)


def base_sum_kernel(keep, got, up, low_got, mine, other, up_held):
    del low_got
    chip_sum_kernel(keep, got, mine, other)
    up_held[...] = up[...]


def lanes(shape, low_rank):
    position = lax.broadcasted_iota(jnp.int32, shape, 1)
    starts = range(low_rank, shape[1], low_rank)
    return sum((position >= start).astype(jnp.int32) for start in starts)


def reduced_kernel(mine, got, slots, up2, out):
    wide = mine.shape[1]
    out[:, :wide] = (mine[...] + got[...]).astype(out.dtype)
    out[:, wide:] = slots[...].astype(jnp.float32).astype(out.dtype)


def hold_kernel(first, second, out0, out1):
    out0[...] = first[...]
    out1[...] = second[...]


def delta_kernel(low_rank, owner0, owner1, owner2, owner3, up0, up1, up2, up3, mine, out):
    t, q = lax.axis_index("tenant"), lax.axis_index("tensor")
    f32, bf16 = jnp.float32, jnp.bfloat16
    wide = up0.shape[0]
    ten_dev = wide // low_rank
    owners = [owner0[...], owner1[...], owner2[...], owner3[...]]
    owners = [owner.astype(f32) for owner in owners]
    tags = sum(jnp.where((t ^ step) == q, owner[:, wide:], 0.0) for step, owner in enumerate(owners))
    slots = jnp.concatenate([tags] * (wide // tags.shape[1]), axis=1).astype(jnp.int32)
    lane = lanes(slots.shape, low_rank)
    chosen = jnp.zeros(slots.shape, f32)
    for step, owner in enumerate(owners):
        chosen = chosen + jnp.where(slots - (t ^ step) * ten_dev == lane, owner[:, :wide], 0.0)
    i = lax.broadcasted_iota(jnp.int32, (wide, wide), 0)
    j = lax.broadcasted_iota(jnp.int32, (wide, wide), 1)
    same = jnp.zeros((wide, wide), f32)
    for shift in range(-wide + low_rank, wide, low_rank):
        same = jnp.where(i - j == shift, 1.0, same)
    spread = dot(chosen.astype(bf16), same.astype(bf16))
    terms = []
    for step, up in zip((0, 2, 1, 3), (up0, up1, up2, up3)):
        here = slots - (q ^ step) * ten_dev == lane
        terms.append((jnp.where(here, spread, 0.0).astype(bf16), up))
    for part in tiles(mine.shape[1]):
        total = mine[:, part]
        for rows, up in terms:
            total = total + dot(rows, up[:, part])
        out[:, part] = total


def on_device_4x4(hidden_states, tenant_ids, owner_map, down_weight, adapter_down, adapter_up):
    rows, depth = hidden_states.shape
    cols = down_weight.shape[1]
    half = depth // 2
    ten_dev, _, low_rank = adapter_down.shape
    wide = ten_dev * low_rank
    bf16, f32 = jnp.bfloat16, jnp.float32

    def along(name, pairs):
        return lambda value: lax.ppermute(value, name, pairs)

    outer_pairs = along("tenant", [(0, 1), (1, 0), (2, 3), (3, 2)])
    two_apart = along("tenant", [(0, 2), (2, 0), (1, 3), (3, 1)])
    inner_pair = along("tenant", [(1, 2), (2, 1)])
    to_ends = along("tenant", [(2, 3), (1, 0)])
    opposite = along("tenant", [(0, 3), (3, 0), (1, 2), (2, 1)])
    cores = along("tensor", [(0, 1), (1, 0), (2, 3), (3, 2)])
    chips = along("tensor", [(0, 2), (2, 0), (1, 3), (3, 1)])

    def out(shape, dtype=f32):
        return jax.ShapeDtypeStruct(shape, dtype)

    tall, flat, part = (rows, cols), (rows, wide), (rows, half)

    two = [two_apart(hidden_states[:, :half]), two_apart(hidden_states[:, half:])]
    pair = outer_pairs(hidden_states)
    up0 = adapter_up.reshape(wide, cols)
    up1 = chips(up0)
    down = jnp.transpose(adapter_down, (0, 2, 1)).reshape(wide, depth)
    base0, low0, *own = call(
        own_kernel,
        [out(tall), out(flat), out(part, bf16), out(part, bf16)],
        hidden_states, down_weight, down,
    )
    end = [to_ends(value) for value in two]
    inner = [inner_pair(value) for value in own]
    base1, base2, low12 = call(
        middle_kernel,
        [out(tall), out(tall), out((2 * rows, wide))],
        pair, *two, down_weight, down,
        scratch=[pltpu.VMEM((2 * rows, depth), bf16)],
    )
    early, low_early = call(
        early_kernel,
        [out(tall), out((2 * rows, wide))],
        end[0], inner[0], down_weight, down, base2, low12,
    )
    low_give, low_keep = call(
        low_kernel, [out((2 * rows, wide))] * 2, end[1], inner[1], down, low0, low12, low_early
    )
    (base3,) = call(late_kernel, [out(tall)], end[1], inner[1], down_weight, early, low_give)
    low_mine, low_other = call(
        low_sum_kernel, [out(flat)] * 2, low_keep, cores(low_give), base3
    )
    low_from_chip = chips(low_other)
    give, keep = call(
        pick_kernel,
        [out((2 * rows, cols), bf16), out((2 * rows, cols))],
        base0, base1, base2, base3, low_other,
    )
    mine, other, up_held = call(
        base_sum_kernel,
        [out(tall), out(tall, bf16), out((wide, cols), bf16)],
        keep, cores(give), up1, low_from_chip,
    )
    from_chip = chips(other)
    up2 = cores(up0)
    slots = jnp.broadcast_to(lookup(tenant_ids, owner_map)[:, None], (rows, 128))
    (reduced,) = call(
        reduced_kernel, [out((rows, wide + 128), bf16)], low_mine, low_from_chip, slots, up2
    )
    shape = out((rows, wide + 128), bf16)
    held, two = call(hold_kernel, [shape] * 2, reduced, two_apart(reduced))
    owners = [held, outer_pairs(reduced), two, opposite(reduced)]
    (total,) = call(
        functools.partial(delta_kernel, low_rank),
        [out(tall)],
        *owners, up0, up1, up2, cores(up_held), mine,
    )
    return (total + from_chip.astype(f32)).astype(bf16)


def solution(mesh):
    small = mesh.shape["tenant"] == 4 and mesh.shape["tensor"] == 4
    return jax.shard_map(
        on_device_4x4 if small else on_device_general,
        mesh=mesh,
        in_specs=(
            P(("groups", "tenant"), "tensor"),
            P(("groups", "tenant")),
            P("groups"),
            P("tensor", "tenant"),
            P(("groups", "tenant"), "tensor", None),
            P(("groups", "tensor"), None, "tenant"),
        ),
        out_specs=P(("groups", "tensor"), "tenant"),
        check_vma=False,
    )
```

```python
import functools

import jax
import jax.numpy as jnp
from jax import lax
from jax.experimental import pallas as pl
from jax.experimental.pallas import tpu as pltpu
from jax.sharding import PartitionSpec as P


def lookup(row_ids, mapping):
    matches = row_ids[:, None] == jnp.arange(mapping.shape[0], dtype=jnp.int32)[None, :]
    return jnp.sum(jnp.where(matches, mapping[None, :], 0), axis=1)


def on_device_general(hidden_states, tenant_ids, owner_map, down_weight, adapter_down, adapter_up):
    rows_dev = hidden_states.shape[0]
    ten_dev = adapter_down.shape[0]
    low_rank = adapter_down.shape[2]
    per_group = adapter_up.shape[0]
    cols_dev = adapter_up.shape[2]
    owners = lax.axis_size("tenant")
    capacity = min(4 * rows_dev // owners, rows_dev // 2)
    slot_limit = owners * capacity
    me_group = lax.axis_index("tensor")
    everyone, all_ids = (
        lax.all_gather(hidden_states, "tenant", axis=0, tiled=True),
        lax.all_gather(tenant_ids, "tenant", axis=0, tiled=True),
    )
    total_rows = everyone.shape[0]
    all_slots = lookup(all_ids, owner_map)
    my_slots = lookup(tenant_ids, owner_map)
    target = my_slots // ten_dev
    onehot = (target[:, None] == jnp.arange(owners, dtype=jnp.int32)[None, :]).astype(jnp.int32)
    position = jnp.sum(jnp.cumsum(onehot, axis=0) * onehot, axis=1) - 1
    slot_cell = target * capacity + position
    select = slot_cell[None, :] == jnp.arange(slot_limit, dtype=jnp.int32)[:, None]
    outgoing = jnp.dot(
        select.astype(jnp.bfloat16), hidden_states, preferred_element_type=jnp.float32
    )
    outgoing = outgoing.astype(jnp.bfloat16).reshape(owners, capacity, hidden_states.shape[1])
    local_tags = jnp.sum(jnp.where(select, (my_slots % ten_dev)[None, :], 0), axis=1)
    local_tags = jnp.where(jnp.any(select, axis=1), local_tags, -1).reshape(owners, capacity)
    payload = lax.all_to_all(outgoing, "tenant", split_axis=0, concat_axis=0, tiled=True)
    project_local_tags = lax.all_to_all(
        local_tags, "tenant", split_axis=0, concat_axis=0, tiled=True
    )
    flattened = payload.reshape(-1, payload.shape[2])
    mixed = jnp.einsum("nf,tfk->ntk", flattened, adapter_down, preferred_element_type=jnp.float32)
    chosen = (
        project_local_tags.reshape(-1)[:, None] == jnp.arange(ten_dev, dtype=jnp.int32)[None, :]
    )
    result = jnp.sum(jnp.where(chosen[:, :, None], mixed, 0.0), axis=1)
    partial_value = result.reshape(payload.shape[0], payload.shape[1], low_rank)
    summed = lax.psum(partial_value, "tensor")
    reduced = lax.all_to_all(
        summed.astype(jnp.bfloat16), "tenant", split_axis=0, concat_axis=0, tiled=True
    )
    my_low = jnp.dot(
        select.T.astype(jnp.bfloat16),
        reduced.reshape(-1, low_rank),
        preferred_element_type=jnp.float32,
    )
    all_low = lax.all_gather(my_low.astype(jnp.bfloat16), "tenant", axis=0, tiled=True)
    first_slot = me_group * per_group
    group_index = all_slots - first_slot
    chosen_group = group_index[:, None] == jnp.arange(per_group, dtype=jnp.int32)[None, :]
    spread = jnp.where(chosen_group[:, :, None], all_low[:, None, :], jnp.zeros((), jnp.bfloat16))
    spread = spread.reshape(total_rows, per_group * low_rank)
    up_flat = adapter_up.reshape(per_group * low_rank, cols_dev)
    layer_out = lax.psum_scatter(
        jnp.dot(everyone, down_weight, preferred_element_type=jnp.float32),
        "tensor",
        scatter_dimension=0,
        tiled=True,
    )
    layer_out = layer_out + lax.psum_scatter(
        jnp.dot(spread, up_flat, preferred_element_type=jnp.float32),
        "tensor",
        scatter_dimension=0,
        tiled=True,
    )
    return layer_out.astype(jnp.bfloat16)


def dot(a, b):
    return jnp.dot(a, b, preferred_element_type=jnp.float32)


def dot_t(a, b):
    return lax.dot_general(a, b, (((1,), (1,)), ((), ())), preferred_element_type=jnp.float32)


LATE = 2**23
CHEAP = pl.CostEstimate(flops=1, bytes_accessed=1, transcendentals=0)
HERE = pl.BlockSpec(memory_space=pltpu.VMEM)
TILE = 256


def call(kernel, outs, *operands, scratch=(), cost=CHEAP):
    return pl.pallas_call(
        kernel,
        in_specs=[HERE] * len(operands),
        out_specs=[HERE] * len(outs),
        out_shape=list(outs),
        scratch_shapes=list(scratch),
        cost_estimate=cost,
        compiler_params=pltpu.CompilerParams(vmem_limit_bytes=8 * 2**20),
    )(*operands)


def tiles(length):
    return [slice(i, i + TILE) for i in range(0, length, TILE)]


def is_even():
    return lax.axis_index("tenant") % 2 == lax.axis_index("tensor") % 2


def is_near():
    return lax.axis_index("tenant") // 2 == lax.axis_index("tensor") // 2


def arrived(end, inner):
    t = lax.axis_index("tenant")
    return jnp.where((t == 1) | (t == 2), inner[...], end[...])


def own_kernel(x, w, down, base0, low0, a, b):
    half = a.shape[1]
    a[...] = x[:, :half]
    b[...] = x[:, half:]
    low0[...] = dot_t(x[...], down[...])
    for part in tiles(w.shape[1]):
        base0[:, part] = dot(x[...], w[:, part])


def middle_kernel(pair, two_a, two_b, w, down, base1, base2, low, both):
    rows, half = two_a.shape
    both[:rows] = pair[...]
    both[rows:, :half] = two_a[...]
    both[rows:, half:] = two_b[...]
    low[...] = dot_t(both[...], down[...])
    for part in tiles(w.shape[1]):
        got = dot(both[...], w[:, part])
        base1[:, part] = got[:rows]
        base2[:, part] = got[rows:]


def early_kernel(end, inner, w, down, base2, low12, early, low_early):
    del base2
    rows, half = end.shape
    x = arrived(end, inner)
    low_early[:rows] = low12[rows:]
    low_early[rows:] = dot_t(x, down[:, :half])
    for part in tiles(w.shape[1]):
        early[:, part] = dot(x, w[:half, part])


def pick(blocks, part, give, keep):
    even = is_even()
    rows = blocks[0].shape[0]
    for at in (0, 1):
        first, second = blocks[2 * at], blocks[2 * at + 1]
        target = slice(at * rows, (at + 1) * rows)
        keep[target, part] = jnp.where(even, first, second)
        give[target, part] = jnp.where(even, second, first).astype(give.dtype)


def low_kernel(end, inner, down, low0, low12, low_early, slots, give, keep):
    del slots
    rows, half = end.shape
    low3 = low_early[rows:] + dot_t(arrived(end, inner), down[:, half:])
    blocks = (low0[...], low12[:rows], low_early[:rows], low3)
    pick(blocks, slice(None), give, keep)


def late_kernel(end, inner, w, early, low_give, base3):
    del low_give
    half = end.shape[1]
    x = arrived(end, inner)
    for part in tiles(w.shape[1]):
        base3[:, part] = early[:, part] + dot(x, w[half:, part])


def pick_kernel(base0, base1, base2, base3, low_other, give, keep):
    del low_other
    for part in tiles(base0.shape[1]):
        pick([block[:, part] for block in (base0, base1, base2, base3)], part, give, keep)


def chip_sum_kernel(keep, got, mine, other):
    near = is_near()
    rows = mine.shape[0]
    for part in tiles(mine.shape[1]):
        both = keep[:, part] + got[:, part].astype(jnp.float32)
        mine[:, part] = jnp.where(near, both[:rows], both[rows:])
        other[:, part] = jnp.where(near, both[rows:], both[:rows]).astype(other.dtype)


def low_sum_kernel(keep, got, base3, mine, other):
    del base3
    chip_sum_kernel(keep, got, mine, other)


def base_sum_kernel(keep, got, up, low_got, mine, other, up_held):
    del low_got
    chip_sum_kernel(keep, got, mine, other)
    up_held[...] = up[...]


def lanes(shape, low_rank):
    position = lax.broadcasted_iota(jnp.int32, shape, 1)
    starts = range(low_rank, shape[1], low_rank)
    return sum((position >= start).astype(jnp.int32) for start in starts)


def reduced_kernel(mine, got, slots, up2, out):
    del up2
    rows = mine.shape[0]
    out[:rows] = (mine[...] + got[...].astype(jnp.float32)).astype(out.dtype)
    out[rows:] = slots[...].astype(jnp.float32).astype(out.dtype)


def hold_kernel(first, second, out0, out1):
    out0[...] = first[...]
    out1[...] = second[...]


def delta_kernel(low_rank, owner0, owner1, owner2, owner3, up0, up1, up2, up3, mine, out):
    t, q = lax.axis_index("tenant"), lax.axis_index("tensor")
    f32, bf16 = jnp.float32, jnp.bfloat16
    wide = up0.shape[0]
    ten_dev = wide // low_rank
    owners = [owner0[...], owner1[...], owner2[...], owner3[...]]
    owners = [owner.astype(f32) for owner in owners]
    rows = mine.shape[0]
    tags = sum(jnp.where((t ^ step) == q, owner[rows:], 0.0) for step, owner in enumerate(owners))
    i = lax.broadcasted_iota(jnp.int32, (rows, wide), 0)
    j = lax.broadcasted_iota(jnp.int32, (rows, wide), 1)
    column = jnp.sum(jnp.where(i == j, tags[:1], 0.0), axis=1, keepdims=True)
    slots = jnp.broadcast_to(column, (rows, wide)).astype(jnp.int32)
    lane = lanes(slots.shape, low_rank)
    chosen = jnp.zeros(slots.shape, f32)
    for step, owner in enumerate(owners):
        chosen = chosen + jnp.where(slots - (t ^ step) * ten_dev == lane, owner[:rows], 0.0)
    i = lax.broadcasted_iota(jnp.int32, (wide, wide), 0)
    j = lax.broadcasted_iota(jnp.int32, (wide, wide), 1)
    same = jnp.zeros((wide, wide), f32)
    for shift in range(-wide + low_rank, wide, low_rank):
        same = jnp.where(i - j == shift, 1.0, same)
    spread = dot(chosen.astype(bf16), same.astype(bf16))
    terms = []
    for step, up in zip((0, 2, 1, 3), (up0, up1, up2, up3)):
        here = slots - (q ^ step) * ten_dev == lane
        terms.append((jnp.where(here, spread, 0.0).astype(bf16), up))
    for part in tiles(mine.shape[1]):
        total = mine[:, part]
        for rows, up in terms:
            total = total + dot(rows, up[:, part])
        out[:, part] = total


def on_device_4x4(hidden_states, tenant_ids, owner_map, down_weight, adapter_down, adapter_up):
    rows, depth = hidden_states.shape
    cols = down_weight.shape[1]
    half = depth // 2
    ten_dev, _, low_rank = adapter_down.shape
    wide = ten_dev * low_rank
    bf16, f32 = jnp.bfloat16, jnp.float32

    def along(name, pairs):
        return lambda value: lax.ppermute(value, name, pairs)

    outer_pairs = along("tenant", [(0, 1), (1, 0), (2, 3), (3, 2)])
    two_apart = along("tenant", [(0, 2), (2, 0), (1, 3), (3, 1)])
    inner_pair = along("tenant", [(1, 2), (2, 1)])
    to_ends = along("tenant", [(2, 3), (1, 0)])
    opposite = along("tenant", [(0, 3), (3, 0), (1, 2), (2, 1)])
    cores = along("tensor", [(0, 1), (1, 0), (2, 3), (3, 2)])
    chips = along("tensor", [(0, 2), (2, 0), (1, 3), (3, 1)])

    def out(shape, dtype=f32):
        return jax.ShapeDtypeStruct(shape, dtype)

    tall, flat, part = (rows, cols), (rows, wide), (rows, half)

    two = [two_apart(hidden_states[:, :half]), two_apart(hidden_states[:, half:])]
    pair = outer_pairs(hidden_states)
    up0 = adapter_up.reshape(wide, cols)
    up1 = chips(up0)
    down = jnp.transpose(adapter_down, (0, 2, 1)).reshape(wide, depth)
    base0, low0, *own = call(
        own_kernel,
        [out(tall), out(flat), out(part, bf16), out(part, bf16)],
        hidden_states, down_weight, down,
    )
    end = [to_ends(value) for value in two]
    inner = [inner_pair(value) for value in own]
    base1, base2, low12 = call(
        middle_kernel,
        [out(tall), out(tall), out((2 * rows, wide))],
        pair, *two, down_weight, down,
        scratch=[pltpu.VMEM((2 * rows, depth), bf16)],
    )
    early, low_early = call(
        early_kernel,
        [out(tall), out((2 * rows, wide))],
        end[0], inner[0], down_weight, down, base2, low12,
    )
    slots = jnp.pad(lookup(tenant_ids, owner_map), (0, wide - rows))
    slots = jnp.broadcast_to(slots[None], (16, wide))
    low_give, low_keep = call(
        low_kernel,
        [out((2 * rows, wide))] * 2,
        end[1], inner[1], down, low0, low12, low_early, slots,
    )
    (base3,) = call(late_kernel, [out(tall)], end[1], inner[1], down_weight, early, low_give)
    low_mine, low_other = call(
        low_sum_kernel, [out(flat), out(flat, bf16)], low_keep, cores(low_give), base3
    )
    low_from_chip = chips(low_other)
    give, keep = call(
        pick_kernel,
        [out((2 * rows, cols), bf16), out((2 * rows, cols))],
        base0, base1, base2, base3, low_other,
    )
    mine, other, up_held = call(
        base_sum_kernel,
        [out(tall), out(tall, bf16), out((wide, cols), bf16)],
        keep, cores(give), up1, low_from_chip,
    )
    from_chip = chips(other)
    up2 = cores(up0)
    shape = out((rows + 16, wide), bf16)
    (reduced,) = call(reduced_kernel, [shape], low_mine, low_from_chip, slots, up2)
    held, two = call(hold_kernel, [shape] * 2, reduced, two_apart(reduced))
    owners = [held, outer_pairs(reduced), two, opposite(reduced)]
    (total,) = call(
        functools.partial(delta_kernel, low_rank),
        [out(tall)],
        *owners, up0, up1, up2, cores(up_held), mine,
    )
    return (total + from_chip.astype(f32)).astype(bf16)


def solution(mesh):
    small = mesh.shape["tenant"] == 4 and mesh.shape["tensor"] == 4
    return jax.shard_map(
        on_device_4x4 if small else on_device_general,
        mesh=mesh,
        in_specs=(
            P(("groups", "tenant"), "tensor"),
            P(("groups", "tenant")),
            P("groups"),
            P("tensor", "tenant"),
            P(("groups", "tenant"), "tensor", None),
            P(("groups", "tensor"), None, "tenant"),
        ),
        out_specs=P(("groups", "tensor"), "tenant"),
        check_vma=False,
    )
```

```python
import functools

import jax
import jax.numpy as jnp
from jax import lax
from jax.experimental import pallas as pl
from jax.experimental.pallas import tpu as pltpu
from jax.sharding import PartitionSpec as P


def lookup(row_ids, mapping):
    matches = row_ids[:, None] == jnp.arange(mapping.shape[0], dtype=jnp.int32)[None, :]
    return jnp.sum(jnp.where(matches, mapping[None, :], 0), axis=1)


def on_device_general(hidden_states, tenant_ids, owner_map, down_weight, adapter_down, adapter_up):
    rows_dev = hidden_states.shape[0]
    ten_dev = adapter_down.shape[0]
    low_rank = adapter_down.shape[2]
    per_group = adapter_up.shape[0]
    cols_dev = adapter_up.shape[2]
    owners = lax.axis_size("tenant")
    capacity = min(4 * rows_dev // owners, rows_dev // 2)
    slot_limit = owners * capacity
    me_group = lax.axis_index("tensor")
    everyone, all_ids = (
        lax.all_gather(hidden_states, "tenant", axis=0, tiled=True),
        lax.all_gather(tenant_ids, "tenant", axis=0, tiled=True),
    )
    total_rows = everyone.shape[0]
    all_slots = lookup(all_ids, owner_map)
    my_slots = lookup(tenant_ids, owner_map)
    target = my_slots // ten_dev
    onehot = (target[:, None] == jnp.arange(owners, dtype=jnp.int32)[None, :]).astype(jnp.int32)
    position = jnp.sum(jnp.cumsum(onehot, axis=0) * onehot, axis=1) - 1
    slot_cell = target * capacity + position
    select = slot_cell[None, :] == jnp.arange(slot_limit, dtype=jnp.int32)[:, None]
    outgoing = jnp.dot(
        select.astype(jnp.bfloat16), hidden_states, preferred_element_type=jnp.float32
    )
    outgoing = outgoing.astype(jnp.bfloat16).reshape(owners, capacity, hidden_states.shape[1])
    local_tags = jnp.sum(jnp.where(select, (my_slots % ten_dev)[None, :], 0), axis=1)
    local_tags = jnp.where(jnp.any(select, axis=1), local_tags, -1).reshape(owners, capacity)
    payload = lax.all_to_all(outgoing, "tenant", split_axis=0, concat_axis=0, tiled=True)
    project_local_tags = lax.all_to_all(
        local_tags, "tenant", split_axis=0, concat_axis=0, tiled=True
    )
    flattened = payload.reshape(-1, payload.shape[2])
    mixed = jnp.einsum("nf,tfk->ntk", flattened, adapter_down, preferred_element_type=jnp.float32)
    chosen = (
        project_local_tags.reshape(-1)[:, None] == jnp.arange(ten_dev, dtype=jnp.int32)[None, :]
    )
    result = jnp.sum(jnp.where(chosen[:, :, None], mixed, 0.0), axis=1)
    partial_value = result.reshape(payload.shape[0], payload.shape[1], low_rank)
    summed = lax.psum(partial_value, "tensor")
    reduced = lax.all_to_all(
        summed.astype(jnp.bfloat16), "tenant", split_axis=0, concat_axis=0, tiled=True
    )
    my_low = jnp.dot(
        select.T.astype(jnp.bfloat16),
        reduced.reshape(-1, low_rank),
        preferred_element_type=jnp.float32,
    )
    all_low = lax.all_gather(my_low.astype(jnp.bfloat16), "tenant", axis=0, tiled=True)
    first_slot = me_group * per_group
    group_index = all_slots - first_slot
    chosen_group = group_index[:, None] == jnp.arange(per_group, dtype=jnp.int32)[None, :]
    spread = jnp.where(chosen_group[:, :, None], all_low[:, None, :], jnp.zeros((), jnp.bfloat16))
    spread = spread.reshape(total_rows, per_group * low_rank)
    up_flat = adapter_up.reshape(per_group * low_rank, cols_dev)
    layer_out = lax.psum_scatter(
        jnp.dot(everyone, down_weight, preferred_element_type=jnp.float32),
        "tensor",
        scatter_dimension=0,
        tiled=True,
    )
    layer_out = layer_out + lax.psum_scatter(
        jnp.dot(spread, up_flat, preferred_element_type=jnp.float32),
        "tensor",
        scatter_dimension=0,
        tiled=True,
    )
    return layer_out.astype(jnp.bfloat16)


def dot(a, b):
    return jnp.dot(a, b, preferred_element_type=jnp.float32)


def dot_t(a, b):
    return lax.dot_general(a, b, (((1,), (1,)), ((), ())), preferred_element_type=jnp.float32)


CHEAP = pl.CostEstimate(flops=1, bytes_accessed=1, transcendentals=0)
HERE = pl.BlockSpec(memory_space=pltpu.VMEM)
TILE = 256


def call(kernel, outs, *operands, scratch=()):
    return pl.pallas_call(
        kernel,
        in_specs=[HERE] * len(operands),
        out_specs=[HERE] * len(outs),
        out_shape=list(outs),
        scratch_shapes=list(scratch),
        cost_estimate=CHEAP,
        compiler_params=pltpu.CompilerParams(vmem_limit_bytes=8 * 2**20),
    )(*operands)


def tiles(length):
    return [slice(i, i + TILE) for i in range(0, length, TILE)]


def is_even():
    return lax.axis_index("tenant") % 2 == lax.axis_index("tensor") % 2


def is_near():
    return lax.axis_index("tenant") // 2 == lax.axis_index("tensor") // 2


def arrived(end, inner):
    t = lax.axis_index("tenant")
    return jnp.where((t == 1) | (t == 2), inner[...], end[...])


def own_kernel(x, w, down, base0, low0, a, b):
    half = a.shape[1]
    a[...] = x[:, :half]
    b[...] = x[:, half:]
    low0[...] = dot_t(x[...], down[...])
    for part in tiles(w.shape[1]):
        base0[:, part] = dot(x[...], w[:, part])


def middle_kernel(pair, two_a, two_b, w, down, base1, base2, low, both):
    rows, half = two_a.shape
    both[:rows] = pair[...]
    both[rows:, :half] = two_a[...]
    both[rows:, half:] = two_b[...]
    low[...] = dot_t(both[...], down[...])
    for part in tiles(w.shape[1]):
        got = dot(both[...], w[:, part])
        base1[:, part] = got[:rows]
        base2[:, part] = got[rows:]


def early_kernel(end, inner, w, down, base2, low12, early, low_early):
    del base2
    rows, half = end.shape
    x = arrived(end, inner)
    low_early[:rows] = low12[rows:]
    low_early[rows:] = dot_t(x, down[:, :half])
    for part in tiles(w.shape[1]):
        early[:, part] = dot(x, w[:half, part])


def pick(blocks, part, give, keep):
    even = is_even()
    rows = blocks[0].shape[0]
    for at in (0, 1):
        first, second = blocks[2 * at], blocks[2 * at + 1]
        target = slice(at * rows, (at + 1) * rows)
        keep[target, part] = jnp.where(even, first, second)
        give[target, part] = jnp.where(even, second, first).astype(give.dtype)


def low_kernel(end, inner, down, low0, low12, low_early, slots, give, keep):
    del slots
    rows, half = end.shape
    low3 = low_early[rows:] + dot_t(arrived(end, inner), down[:, half:])
    blocks = (low0[...], low12[:rows], low_early[:rows], low3)
    pick(blocks, slice(None), give, keep)


def late_kernel(end, inner, w, early, low_give, base3):
    del low_give
    half = end.shape[1]
    x = arrived(end, inner)
    for part in tiles(w.shape[1]):
        base3[:, part] = early[:, part] + dot(x, w[half:, part])


def pick_kernel(base0, base1, base2, base3, low_other, give, keep):
    del low_other
    for part in tiles(base0.shape[1]):
        pick([block[:, part] for block in (base0, base1, base2, base3)], part, give, keep)


def chip_sum_kernel(keep, got, mine, other):
    near = is_near()
    rows = mine.shape[0]
    for part in tiles(mine.shape[1]):
        both = keep[:, part] + got[:, part].astype(jnp.float32)
        mine[:, part] = jnp.where(near, both[:rows], both[rows:])
        other[:, part] = jnp.where(near, both[rows:], both[:rows]).astype(other.dtype)


def low_sum_kernel(keep, got, base3, mine, other):
    del base3
    chip_sum_kernel(keep, got, mine, other)


def base_sum_kernel(keep, got, up, low_got, mine, other, up_held):
    del low_got
    chip_sum_kernel(keep, got, mine, other)
    up_held[...] = up[...]


def lanes(shape, low_rank):
    position = lax.broadcasted_iota(jnp.int32, shape, 1)
    starts = range(low_rank, shape[1], low_rank)
    return sum((position >= start).astype(jnp.int32) for start in starts)


def reduced_kernel(mine, got, slots, up2, out):
    del up2
    rows = mine.shape[0]
    out[:rows] = (mine[...] + got[...].astype(jnp.float32)).astype(out.dtype)
    out[rows:] = slots[...].astype(jnp.float32).astype(out.dtype)


def hold_kernel(first, second, out0, out1):
    out0[...] = first[...]
    out1[...] = second[...]


def delta_kernel(low_rank, owner0, owner1, owner2, owner3, up0, up1, up2, up3, mine, got, out):
    t, q = lax.axis_index("tenant"), lax.axis_index("tensor")
    f32, bf16 = jnp.float32, jnp.bfloat16
    wide = up0.shape[0]
    ten_dev = wide // low_rank
    owners = [owner0[...], owner1[...], owner2[...], owner3[...]]
    owners = [owner.astype(f32) for owner in owners]
    rows = mine.shape[0]
    tags = sum(jnp.where((t ^ step) == q, owner[rows:], 0.0) for step, owner in enumerate(owners))
    i = lax.broadcasted_iota(jnp.int32, (rows, wide), 0)
    j = lax.broadcasted_iota(jnp.int32, (rows, wide), 1)
    column = jnp.sum(jnp.where(i == j, tags[:1], 0.0), axis=1, keepdims=True)
    slots = jnp.broadcast_to(column, (rows, wide)).astype(jnp.int32)
    lane = lanes(slots.shape, low_rank)
    kept = [
        jnp.where(slots - (t ^ step) * ten_dev == lane, owner[:rows], 0.0)
        for step, owner in enumerate(owners)
    ]
    terms = []
    for step, up in zip((0, 2, 1, 3), (up0, up1, up2, up3)):
        mixed = sum(jnp.where((t ^ at) == (q ^ step), value, 0.0) for at, value in enumerate(kept))
        terms.append((mixed.astype(bf16), up))
    for part in tiles(mine.shape[1]):
        total = mine[:, part] + got[:, part].astype(f32)
        for rows, up in terms:
            total = total + dot(rows, up[:, part])
        out[:, part] = total.astype(out.dtype)


def on_device_4x4(hidden_states, tenant_ids, owner_map, down_weight, adapter_down, adapter_up):
    rows, depth = hidden_states.shape
    cols = down_weight.shape[1]
    half = depth // 2
    ten_dev, _, low_rank = adapter_down.shape
    wide = ten_dev * low_rank
    bf16, f32 = jnp.bfloat16, jnp.float32

    def along(name, pairs):
        return lambda value: lax.ppermute(value, name, pairs)

    outer_pairs = along("tenant", [(0, 1), (1, 0), (2, 3), (3, 2)])
    two_apart = along("tenant", [(0, 2), (2, 0), (1, 3), (3, 1)])
    inner_pair = along("tenant", [(1, 2), (2, 1)])
    to_ends = along("tenant", [(2, 3), (1, 0)])
    opposite = along("tenant", [(0, 3), (3, 0), (1, 2), (2, 1)])
    cores = along("tensor", [(0, 1), (1, 0), (2, 3), (3, 2)])
    chips = along("tensor", [(0, 2), (2, 0), (1, 3), (3, 1)])

    def out(shape, dtype=f32):
        return jax.ShapeDtypeStruct(shape, dtype)

    tall, flat, part = (rows, cols), (rows, wide), (rows, half)

    two = [two_apart(hidden_states[:, :half]), two_apart(hidden_states[:, half:])]
    pair = outer_pairs(hidden_states)
    up0 = adapter_up.reshape(wide, cols)
    up1 = chips(up0)
    down = jnp.transpose(adapter_down, (0, 2, 1)).reshape(wide, depth)
    base0, low0, *own = call(
        own_kernel,
        [out(tall), out(flat), out(part, bf16), out(part, bf16)],
        hidden_states, down_weight, down,
    )
    end = [to_ends(value) for value in two]
    inner = [inner_pair(value) for value in own]
    base1, base2, low12 = call(
        middle_kernel,
        [out(tall), out(tall), out((2 * rows, wide))],
        pair, *two, down_weight, down,
        scratch=[pltpu.VMEM((2 * rows, depth), bf16)],
    )
    early, low_early = call(
        early_kernel,
        [out(tall), out((2 * rows, wide))],
        end[0], inner[0], down_weight, down, base2, low12,
    )
    slots = jnp.pad(lookup(tenant_ids, owner_map), (0, wide - rows))
    slots = jnp.broadcast_to(slots[None], (16, wide))
    low_give, low_keep = call(
        low_kernel,
        [out((2 * rows, wide))] * 2,
        end[1], inner[1], down, low0, low12, low_early, slots,
    )
    (base3,) = call(late_kernel, [out(tall)], end[1], inner[1], down_weight, early, low_give)
    low_mine, low_other = call(
        low_sum_kernel, [out(flat), out(flat, bf16)], low_keep, cores(low_give), base3
    )
    low_from_chip = chips(low_other)
    give, keep = call(
        pick_kernel,
        [out((2 * rows, cols), bf16), out((2 * rows, cols))],
        base0, base1, base2, base3, low_other,
    )
    mine, other, up_held = call(
        base_sum_kernel,
        [out(tall), out(tall, bf16), out((wide, cols), bf16)],
        keep, cores(give), up1, low_from_chip,
    )
    from_chip = chips(other)
    up2 = cores(up0)
    shape = out((rows + 16, wide), bf16)
    (reduced,) = call(reduced_kernel, [shape], low_mine, low_from_chip, slots, up2)
    held, two = call(hold_kernel, [shape] * 2, reduced, two_apart(reduced))
    owners = [held, outer_pairs(reduced), two, opposite(reduced)]
    (total,) = call(
        functools.partial(delta_kernel, low_rank),
        [out(tall, bf16)],
        *owners, up0, up1, up2, cores(up_held), mine, from_chip,
    )
    return total


def solution(mesh):
    small = mesh.shape["tenant"] == 4 and mesh.shape["tensor"] == 4
    return jax.shard_map(
        on_device_4x4 if small else on_device_general,
        mesh=mesh,
        in_specs=(
            P(("groups", "tenant"), "tensor"),
            P(("groups", "tenant")),
            P("groups"),
            P("tensor", "tenant"),
            P(("groups", "tenant"), "tensor", None),
            P(("groups", "tensor"), None, "tenant"),
        ),
        out_specs=P(("groups", "tensor"), "tenant"),
        check_vma=False,
    )
```

```python
import functools

import jax
import jax.numpy as jnp
from jax import lax
from jax.experimental import pallas as pl
from jax.experimental.pallas import tpu as pltpu
from jax.sharding import PartitionSpec as P


def lookup(row_ids, mapping):
    matches = row_ids[:, None] == jnp.arange(mapping.shape[0], dtype=jnp.int32)[None, :]
    return jnp.sum(jnp.where(matches, mapping[None, :], 0), axis=1)


def on_device_general(hidden_states, tenant_ids, owner_map, down_weight, adapter_down, adapter_up):
    rows_dev = hidden_states.shape[0]
    ten_dev = adapter_down.shape[0]
    low_rank = adapter_down.shape[2]
    per_group = adapter_up.shape[0]
    cols_dev = adapter_up.shape[2]
    owners = lax.axis_size("tenant")
    capacity = min(4 * rows_dev // owners, rows_dev // 2)
    slot_limit = owners * capacity
    me_group = lax.axis_index("tensor")
    everyone, all_ids = (
        lax.all_gather(hidden_states, "tenant", axis=0, tiled=True),
        lax.all_gather(tenant_ids, "tenant", axis=0, tiled=True),
    )
    total_rows = everyone.shape[0]
    all_slots = lookup(all_ids, owner_map)
    my_slots = lookup(tenant_ids, owner_map)
    target = my_slots // ten_dev
    onehot = (target[:, None] == jnp.arange(owners, dtype=jnp.int32)[None, :]).astype(jnp.int32)
    position = jnp.sum(jnp.cumsum(onehot, axis=0) * onehot, axis=1) - 1
    slot_cell = target * capacity + position
    select = slot_cell[None, :] == jnp.arange(slot_limit, dtype=jnp.int32)[:, None]
    outgoing = jnp.dot(
        select.astype(jnp.bfloat16), hidden_states, preferred_element_type=jnp.float32
    )
    outgoing = outgoing.astype(jnp.bfloat16).reshape(owners, capacity, hidden_states.shape[1])
    local_tags = jnp.sum(jnp.where(select, (my_slots % ten_dev)[None, :], 0), axis=1)
    local_tags = jnp.where(jnp.any(select, axis=1), local_tags, -1).reshape(owners, capacity)
    payload = lax.all_to_all(outgoing, "tenant", split_axis=0, concat_axis=0, tiled=True)
    project_local_tags = lax.all_to_all(
        local_tags, "tenant", split_axis=0, concat_axis=0, tiled=True
    )
    flattened = payload.reshape(-1, payload.shape[2])
    mixed = jnp.einsum("nf,tfk->ntk", flattened, adapter_down, preferred_element_type=jnp.float32)
    chosen = (
        project_local_tags.reshape(-1)[:, None] == jnp.arange(ten_dev, dtype=jnp.int32)[None, :]
    )
    result = jnp.sum(jnp.where(chosen[:, :, None], mixed, 0.0), axis=1)
    partial_value = result.reshape(payload.shape[0], payload.shape[1], low_rank)
    summed = lax.psum(partial_value, "tensor")
    reduced = lax.all_to_all(
        summed.astype(jnp.bfloat16), "tenant", split_axis=0, concat_axis=0, tiled=True
    )
    my_low = jnp.dot(
        select.T.astype(jnp.bfloat16),
        reduced.reshape(-1, low_rank),
        preferred_element_type=jnp.float32,
    )
    all_low = lax.all_gather(my_low.astype(jnp.bfloat16), "tenant", axis=0, tiled=True)
    first_slot = me_group * per_group
    group_index = all_slots - first_slot
    chosen_group = group_index[:, None] == jnp.arange(per_group, dtype=jnp.int32)[None, :]
    spread = jnp.where(chosen_group[:, :, None], all_low[:, None, :], jnp.zeros((), jnp.bfloat16))
    spread = spread.reshape(total_rows, per_group * low_rank)
    up_flat = adapter_up.reshape(per_group * low_rank, cols_dev)
    layer_out = lax.psum_scatter(
        jnp.dot(everyone, down_weight, preferred_element_type=jnp.float32),
        "tensor",
        scatter_dimension=0,
        tiled=True,
    )
    layer_out = layer_out + lax.psum_scatter(
        jnp.dot(spread, up_flat, preferred_element_type=jnp.float32),
        "tensor",
        scatter_dimension=0,
        tiled=True,
    )
    return layer_out.astype(jnp.bfloat16)


def dot(a, b):
    return jnp.dot(a, b, preferred_element_type=jnp.float32)


def dot_t(a, b):
    return lax.dot_general(a, b, (((1,), (1,)), ((), ())), preferred_element_type=jnp.float32)


CHEAP = pl.CostEstimate(flops=1, bytes_accessed=1, transcendentals=0)
HERE = pl.BlockSpec(memory_space=pltpu.VMEM)
TILE = 256


def call(kernel, outs, *operands, scratch=()):
    return pl.pallas_call(
        kernel,
        in_specs=[HERE] * len(operands),
        out_specs=[HERE] * len(outs),
        out_shape=list(outs),
        scratch_shapes=list(scratch),
        cost_estimate=CHEAP,
        compiler_params=pltpu.CompilerParams(vmem_limit_bytes=8 * 2**20),
    )(*operands)


def tiles(length):
    return [slice(i, i + TILE) for i in range(0, length, TILE)]


def is_even():
    return lax.axis_index("tenant") % 2 == lax.axis_index("tensor") % 2


def is_near():
    return lax.axis_index("tenant") // 2 == lax.axis_index("tensor") // 2


def arrived(end, inner):
    t = lax.axis_index("tenant")
    return jnp.where((t == 1) | (t == 2), inner[...], end[...])


def own_kernel(x, w, down, base0, low0, a, b):
    half = a.shape[1]
    a[...] = x[:, :half]
    b[...] = x[:, half:]
    low0[...] = dot_t(x[...], down[...])
    for part in tiles(w.shape[1]):
        base0[:, part] = dot(x[...], w[:, part])


def middle_kernel(pair, two_a, two_b, w, down, base1, base2, low, both):
    rows, half = two_a.shape
    both[:rows] = pair[...]
    both[rows:, :half] = two_a[...]
    both[rows:, half:] = two_b[...]
    low[...] = dot_t(both[...], down[...])
    for part in tiles(w.shape[1]):
        got = dot(both[...], w[:, part])
        base1[:, part] = got[:rows]
        base2[:, part] = got[rows:]


def early_kernel(end, inner, w, down, base2, low12, early, low_early):
    del base2
    rows, half = end.shape
    x = arrived(end, inner)
    low_early[:rows] = low12[rows:]
    low_early[rows:] = dot_t(x, down[:, :half])
    for part in tiles(w.shape[1]):
        early[:, part] = dot(x, w[:half, part])


def pick(blocks, part, give, keep):
    even = is_even()
    rows = blocks[0].shape[0]
    for at in (0, 1):
        first, second = blocks[2 * at], blocks[2 * at + 1]
        target = slice(at * rows, (at + 1) * rows)
        keep[target, part] = jnp.where(even, first, second)
        give[target, part] = jnp.where(even, second, first).astype(give.dtype)


def low_kernel(end, inner, down, low0, low12, low_early, slots, give, keep):
    del slots
    rows, half = end.shape
    low3 = low_early[rows:] + dot_t(arrived(end, inner), down[:, half:])
    blocks = (low0[...], low12[:rows], low_early[:rows], low3)
    pick(blocks, slice(None), give, keep)


def late_kernel(end, inner, w, early, low_give, base3):
    del low_give
    half = end.shape[1]
    x = arrived(end, inner)
    for part in tiles(w.shape[1]):
        base3[:, part] = early[:, part] + dot(x, w[half:, part])


def pick_kernel(base0, base1, base2, base3, low_other, give, keep):
    del low_other
    for part in tiles(base0.shape[1]):
        pick([block[:, part] for block in (base0, base1, base2, base3)], part, give, keep)


def chip_sum_kernel(keep, got, mine, other):
    near = is_near()
    rows = mine.shape[0]
    for part in tiles(mine.shape[1]):
        both = keep[:, part] + got[:, part].astype(jnp.float32)
        mine[:, part] = jnp.where(near, both[:rows], both[rows:])
        other[:, part] = jnp.where(near, both[rows:], both[:rows]).astype(other.dtype)


def low_sum_kernel(keep, got, base3, mine, other):
    del base3
    chip_sum_kernel(keep, got, mine, other)


def base_sum_kernel(keep, got, up, low_got, mine, other, up_held):
    del low_got
    chip_sum_kernel(keep, got, mine, other)
    up_held[...] = up[...]


def lanes(shape, low_rank):
    position = lax.broadcasted_iota(jnp.int32, shape, 1)
    starts = range(low_rank, shape[1], low_rank)
    return sum((position >= start).astype(jnp.int32) for start in starts)


def reduced_kernel(mine, got, slots, up2, out):
    del up2
    rows = mine.shape[0]
    out[:rows] = (mine[...] + got[...].astype(jnp.float32)).astype(out.dtype)
    out[rows:] = slots[...].astype(jnp.float32).astype(out.dtype)


def delta_kernel(low_rank, owner0, owner1, owner2, owner3, up0, up1, up2, up3, mine, got, out):
    t, q = lax.axis_index("tenant"), lax.axis_index("tensor")
    f32, bf16 = jnp.float32, jnp.bfloat16
    wide = up0.shape[0]
    ten_dev = wide // low_rank
    owners = [owner0[...], owner1[...], owner2[...], owner3[...]]
    owners = [owner.astype(f32) for owner in owners]
    rows = mine.shape[0]
    tags = sum(jnp.where((t ^ step) == q, owner[rows:], 0.0) for step, owner in enumerate(owners))
    i = lax.broadcasted_iota(jnp.int32, (rows, wide), 0)
    j = lax.broadcasted_iota(jnp.int32, (rows, wide), 1)
    column = jnp.sum(jnp.where(i == j, tags[:1], 0.0), axis=1, keepdims=True)
    slots = jnp.broadcast_to(column, (rows, wide)).astype(jnp.int32)
    lane = lanes(slots.shape, low_rank)
    kept = [
        jnp.where(slots - (t ^ step) * ten_dev == lane, owner[:rows], 0.0)
        for step, owner in enumerate(owners)
    ]
    terms = []
    for step, up in zip((0, 2, 1, 3), (up0, up1, up2, up3)):
        mixed = sum(jnp.where((t ^ at) == (q ^ step), value, 0.0) for at, value in enumerate(kept))
        terms.append((mixed.astype(bf16), up))
    for part in tiles(mine.shape[1]):
        total = mine[:, part] + got[:, part].astype(f32)
        for rows, up in terms:
            total = total + dot(rows, up[:, part])
        out[:, part] = total.astype(out.dtype)


def on_device_4x4(hidden_states, tenant_ids, owner_map, down_weight, adapter_down, adapter_up):
    rows, depth = hidden_states.shape
    cols = down_weight.shape[1]
    half = depth // 2
    ten_dev, _, low_rank = adapter_down.shape
    wide = ten_dev * low_rank
    bf16, f32 = jnp.bfloat16, jnp.float32

    def along(name, pairs):
        return lambda value: lax.ppermute(value, name, pairs)

    outer_pairs = along("tenant", [(0, 1), (1, 0), (2, 3), (3, 2)])
    two_apart = along("tenant", [(0, 2), (2, 0), (1, 3), (3, 1)])
    inner_pair = along("tenant", [(1, 2), (2, 1)])
    to_ends = along("tenant", [(2, 3), (1, 0)])
    opposite = along("tenant", [(0, 3), (3, 0), (1, 2), (2, 1)])
    cores = along("tensor", [(0, 1), (1, 0), (2, 3), (3, 2)])
    chips = along("tensor", [(0, 2), (2, 0), (1, 3), (3, 1)])

    def out(shape, dtype=f32):
        return jax.ShapeDtypeStruct(shape, dtype)

    tall, flat, part = (rows, cols), (rows, wide), (rows, half)

    two = [two_apart(hidden_states[:, :half]), two_apart(hidden_states[:, half:])]
    pair = outer_pairs(hidden_states)
    up0 = adapter_up.reshape(wide, cols)
    up1 = chips(up0)
    down = jnp.transpose(adapter_down, (0, 2, 1)).reshape(wide, depth)
    base0, low0, *own = call(
        own_kernel,
        [out(tall), out(flat), out(part, bf16), out(part, bf16)],
        hidden_states, down_weight, down,
    )
    end = [to_ends(value) for value in two]
    inner = [inner_pair(value) for value in own]
    base1, base2, low12 = call(
        middle_kernel,
        [out(tall), out(tall), out((2 * rows, wide))],
        pair, *two, down_weight, down,
        scratch=[pltpu.VMEM((2 * rows, depth), bf16)],
    )
    early, low_early = call(
        early_kernel,
        [out(tall), out((2 * rows, wide))],
        end[0], inner[0], down_weight, down, base2, low12,
    )
    slots = jnp.pad(lookup(tenant_ids, owner_map), (0, wide - rows))
    slots = jnp.broadcast_to(slots[None], (16, wide))
    low_give, low_keep = call(
        low_kernel,
        [out((2 * rows, wide))] * 2,
        end[1], inner[1], down, low0, low12, low_early, slots,
    )
    (base3,) = call(late_kernel, [out(tall)], end[1], inner[1], down_weight, early, low_give)
    low_mine, low_other = call(
        low_sum_kernel, [out(flat), out(flat, bf16)], low_keep, cores(low_give), base3
    )
    low_from_chip = chips(low_other)
    give, keep = call(
        pick_kernel,
        [out((2 * rows, cols), bf16), out((2 * rows, cols))],
        base0, base1, base2, base3, low_other,
    )
    mine, other, up_held = call(
        base_sum_kernel,
        [out(tall), out(tall, bf16), out((wide, cols), bf16)],
        keep, cores(give), up1, low_from_chip,
    )
    from_chip = chips(other)
    up2 = cores(up0)
    shape = out((rows + 16, wide), bf16)
    (reduced,) = call(reduced_kernel, [shape], low_mine, low_from_chip, slots, up2)
    owners = [reduced, outer_pairs(reduced), two_apart(reduced), opposite(reduced)]
    (total,) = call(
        functools.partial(delta_kernel, low_rank),
        [out(tall, bf16)],
        *owners, up0, up1, up2, cores(up_held), mine, from_chip,
    )
    return total


def solution(mesh):
    small = mesh.shape["tenant"] == 4 and mesh.shape["tensor"] == 4
    return jax.shard_map(
        on_device_4x4 if small else on_device_general,
        mesh=mesh,
        in_specs=(
            P(("groups", "tenant"), "tensor"),
            P(("groups", "tenant")),
            P("groups"),
            P("tensor", "tenant"),
            P(("groups", "tenant"), "tensor", None),
            P(("groups", "tensor"), None, "tenant"),
        ),
        out_specs=P(("groups", "tensor"), "tenant"),
        check_vma=False,
    )
```
